32 devices in a mesh: row: 4 (over y, core), col: 8 (over z, x).
Axes of the slice: x: 2, y: 2, z: 4, core: 2. Of those that a mesh axis runs over, the one named last changes fastest.
Arguments:
- x_slots: bfloat16 [4, 16, 128, 128, 128], P('row', 'col'), may hold values from -0.875 to 0.875
- block_pairs: int32 [4, 16], replicated, may hold values from -1 to 15, as said below
- greens: bfloat16 [2, 512, 512], replicated, may hold values from -0.25 to 0.25
- green_mask: int32 [2, 4, 4], replicated, may hold values 0 or 1
- chi_mask: int32 [4, 4], P('row'), may hold values 0 or 1
Outputs:
- chi_blocks: float32 [512, 512], P(('row', 'col'))
The draws below stay inside these ranges and needn't reach their ends.
Inputs may be any that keep to these rules, and one draw needn't show every extreme that they name: `block_pairs`: in each row exactly 10 slots name basis-pair blocks, all different, and all other slots are -1; in every row, all 2 slots of some col index are named.
All inputs are finite; a program needn't handle non-finite values. No bound on the sum of `chi_mask` on one device may be relied on, other than what follows from the above.
Results may differ from the reference program's by a relative error of at most 0.0041.
Values may be sent and summed in bfloat16 or wider, within the bound.
A program may use at most 128 MiB of HBM per device.

```python
import jax
import jax.numpy as jnp
from jax import lax

B = 128
AB = 128
NBLK = 4
NBAS = 512
NAUX = 512
NNZ = 10
SLOTS = 2
N_ROW = 4
N_COL = 8


def draw_block_pairs(key, part):
    row_keys = jax.random.split(key, N_ROW)

    def one_row(row_key):
        first_key, second_key, third_key = jax.random.split(row_key, 3)
        total = N_COL * SLOTS
        filled_owner = jax.random.randint(first_key, (), 0, N_COL)
        priority = jax.random.permutation(second_key, total).astype(jnp.int32)
        owner = jnp.arange(total, dtype=jnp.int32) // SLOTS
        score = jnp.where(owner == filled_owner, priority - total, priority)
        order = jnp.argsort(score, stable=True)
        placing = jnp.argsort(order, stable=True).astype(jnp.int32)
        shuffled = jax.random.permutation(third_key, NBLK * NBLK).astype(jnp.int32)
        picked = shuffled[jnp.minimum(placing, NBLK * NBLK - 1)]
        return jnp.where(placing < NNZ, picked, -1).astype(jnp.int32)
    return jax.vmap(one_row)(row_keys)


def touch_ends(result, own_key, smallest, largest):
    index_at = [jax.random.randint(jax.random.fold_in(own_key, axis), (), 0, length) for axis, length in enumerate(result.shape)]
    widest = result.shape.index(max(result.shape))
    neighbour = index_at[:widest] + [(index_at[widest] + 1) % result.shape[widest]] + index_at[widest + 1:]
    return result.at[tuple(index_at)].set(smallest).at[tuple(neighbour)].set(largest)


def steps_of(own_key, extent, shards, least, top_value):
    level, own = 1.0, jax.random.fold_in(own_key, 6)
    for axis_at, blocks in shards:
        draws = jnp.exp(jax.random.uniform(jax.random.fold_in(own, axis_at), (blocks,), jnp.float32, least / len(shards), top_value / len(shards)))
        level = level * jnp.repeat(draws, extent[axis_at] // blocks).reshape([-1 if axis == axis_at else 1 for axis in range(len(extent))])
    return level


def centred(rng, shape, scale, bound, pieces=(), kind=jnp.bfloat16):
    values = jax.random.normal(rng, shape, jnp.float32) * scale
    if len(pieces) > 0:
        values = steps_of(rng, shape, pieces, -0.22, 0.18) * values
    return jnp.clip(values, min=-bound, max=bound).astype(kind)


def setup_inputs(seed: int = 0) -> dict:
    seeds = jax.random.split(jax.random.key(seed), 6)
    x_slots = centred(seeds[0], (N_ROW, N_COL * SLOTS, AB, B, B), (1.4 / (NBLK * B) ** 0.5), 0.875, ((0, 4), (1, 8)))
    block_pairs = draw_block_pairs(jax.random.fold_in(seeds[5], 71), 0)
    greens = centred(seeds[2], (2, NBAS, NBAS), NBAS ** -0.5, 0.25)
    green_mask = touch_ends((jax.random.randint(seeds[3], (2, NBLK, NBLK), 0, 4) < 3).astype(jnp.int32), jax.random.fold_in(seeds[3], 1), 0, 1)
    chi_mask = touch_ends((jax.random.randint(seeds[4], (N_ROW, N_ROW), 0, 4) < 3).astype(jnp.int32), jax.random.fold_in(seeds[4], 1), 0, 1)
    return dict(x_slots=x_slots, block_pairs=block_pairs, greens=greens, green_mask=green_mask, chi_mask=chi_mask)


def assemble(stored, pair_list):
    selector = (pair_list[:, None] == jnp.arange(NBLK * NBLK, dtype=jnp.int32)[None, :]).astype(jnp.float32)
    pair_blocks = jnp.einsum('kq,kabc->qabc', selector, stored.astype(jnp.float32))
    pair_blocks = pair_blocks.reshape(NBLK, NBLK, AB, B, B).transpose(2, 0, 3, 1, 4)
    return pair_blocks.reshape(AB, NBLK * B, NBLK * B).astype(jnp.bfloat16)


def reference(x_slots, block_pairs, greens, green_mask, chi_mask):
    basis_count = NBLK * B
    full_mask = jnp.repeat(jnp.repeat(green_mask, B, axis=1), B, axis=2).astype(jnp.bfloat16)
    masked = greens * full_mask
    occupied = masked[0].astype(jnp.float32)
    virtual = masked[1].astype(jnp.float32)

    def one_group(operands):
        stored, pair_list = operands
        dense_x = assemble(stored, pair_list)
        half_done = jnp.einsum('ml,pmn->pln', occupied, dense_x.astype(jnp.float32)).astype(jnp.bfloat16)
        contracted = jnp.einsum('pln,ns->pls', half_done.astype(jnp.float32), virtual).astype(jnp.bfloat16)
        return contracted.reshape(AB, basis_count * basis_count), dense_x.reshape(AB, basis_count * basis_count)

    contracted_all, dense_all = lax.map(one_group, (x_slots, block_pairs))
    contracted_all = contracted_all.reshape(NAUX, basis_count * basis_count)
    dense_all = dense_all.reshape(NAUX, basis_count * basis_count)
    chi_sum = lax.dot_general(contracted_all, dense_all, (((1,), (1,)), ((), ())), preferred_element_type=jnp.float32)
    keep = jnp.repeat(jnp.repeat(chi_mask, AB, axis=0), AB, axis=1).astype(jnp.float32)
    return chi_sum * keep
```

```python
import jax
import jax.numpy as jnp
from jax import lax
from jax.sharding import PartitionSpec as P

B = 128
AB = 128
NBLK = 4
NNZ = 10


def on_device(x_slots, block_pairs, greens, green_mask, chi_mask):
    row_count = lax.axis_size("row")
    col_count = lax.axis_size("col")
    dev_count = row_count * col_count
    basis_count = NBLK * B
    pair_total = NBLK * NBLK
    row_index = lax.axis_index("row")
    arrived = lax.all_to_all(x_slots[0], "col", split_axis=1, concat_axis=0, tiled=True)
    aux_local = arrived.shape[1]
    pair_list = lax.dynamic_index_in_dim(block_pairs, row_index, 0, keepdims=False)
    selector = (pair_list[:, None] == jnp.arange(pair_total, dtype=jnp.int32)[None, :]).astype(
        jnp.bfloat16
    )
    pair_blocks = jnp.einsum(
        "kq,kabc->qabc", selector, arrived, preferred_element_type=jnp.float32
    ).astype(jnp.bfloat16)
    dense_x = pair_blocks.reshape(NBLK, NBLK, aux_local, B, B).transpose(2, 0, 3, 1, 4)
    dense_x = dense_x.reshape(aux_local, basis_count, basis_count)
    full_mask = jnp.repeat(jnp.repeat(green_mask, B, axis=1), B, axis=2).astype(jnp.bfloat16)
    masked = greens * full_mask
    half_done = jnp.einsum(
        "ml,pmn->pln", masked[0], dense_x, preferred_element_type=jnp.float32
    ).astype(jnp.bfloat16)
    contracted = jnp.einsum(
        "pln,ns->pls", half_done, masked[1], preferred_element_type=jnp.float32
    ).astype(jnp.bfloat16)
    aux_total = dev_count * aux_local
    named_flag = (block_pairs >= 0).astype(jnp.int32)
    slot_index = jnp.arange(named_flag.shape[1], dtype=jnp.int32)
    not_later = (slot_index[None, :] <= slot_index[:, None]).astype(jnp.int32)
    position = jnp.sum(named_flag[:, None, :] * not_later[None, :, :], axis=2) - 1
    compact_hit = (position[:, None, :] == jnp.arange(NNZ, dtype=jnp.int32)[None, :, None]) & (
        named_flag[:, None, :] > 0
    )
    compact_sel = compact_hit.astype(jnp.int32)
    named_pairs = jnp.sum(compact_sel * block_pairs[:, None, :], axis=2)
    own_sel = lax.dynamic_index_in_dim(compact_sel, row_index, 0, keepdims=False).astype(
        jnp.bfloat16
    )
    block_span = B * B // dev_count
    x_compact = jnp.einsum(
        "js,sabc->ajbc", own_sel, arrived, preferred_element_type=jnp.float32
    ).astype(jnp.bfloat16)
    x_compact = x_compact.reshape(aux_local, NNZ, dev_count, block_span)
    image_blocks = contracted.reshape(aux_local, NBLK, B, NBLK, B).transpose(0, 1, 3, 2, 4)
    image_blocks = image_blocks.reshape(aux_local, pair_total, dev_count, block_span)
    image_rows, compact_rows = (
        lax.all_to_all(image_blocks, ("row", "col"), split_axis=2, concat_axis=0, tiled=True),
        lax.all_to_all(x_compact, ("row", "col"), split_axis=2, concat_axis=0, tiled=True),
    )
    expand = (
        named_pairs[:, :, None] == jnp.arange(pair_total, dtype=jnp.int32)[None, None, :]
    ).astype(jnp.bfloat16)
    compact_rows = compact_rows.reshape(row_count, aux_total // row_count, NNZ, block_span)
    dense_rows = jnp.einsum(
        "rjk,rqjz->rqkz", expand, compact_rows, preferred_element_type=jnp.float32
    ).astype(jnp.bfloat16)
    image_rows = image_rows.reshape(aux_total, pair_total * block_span)
    dense_rows = dense_rows.reshape(aux_total, pair_total * block_span)
    chi_part = lax.dot_general(
        image_rows, dense_rows, (((1,), (1,)), ((), ())), preferred_element_type=jnp.float32
    )
    chi_parts = lax.all_to_all(
        chi_part.reshape(dev_count, aux_local, aux_total),
        ("row", "col"),
        split_axis=0,
        concat_axis=0,
        tiled=True,
    )
    chi_rows = jnp.sum(chi_parts, axis=0)
    column_mask = jnp.repeat(chi_mask[0], AB).astype(jnp.float32)
    return chi_rows * column_mask[None, :]


def solution(mesh):
    in_specs = (P("row", "col", None, None, None), P(), P(), P(), P("row", None))
    out_specs = P(("row", "col"), None)
    return jax.shard_map(
        on_device, mesh=mesh, in_specs=in_specs, out_specs=out_specs, check_vma=False
    )
```

```python
import jax
import jax.numpy as jnp
from jax import lax
from jax.sharding import PartitionSpec as P

B = 128
AB = 128
NBLK = 4
NNZ = 10
CHUNKS = 2


def on_device(x_slots, block_pairs, greens, green_mask, chi_mask):
    row_count = lax.axis_size("row")
    col_count = lax.axis_size("col")
    dev_count = row_count * col_count
    basis_count = NBLK * B
    pair_total = NBLK * NBLK
    row_index = lax.axis_index("row")
    slots = x_slots[0]
    chunk = slots.shape[1] // (col_count * CHUNKS)
    grouped = slots.reshape(slots.shape[0], col_count, CHUNKS, chunk, B, B)
    arrivals = [
        lax.all_to_all(
            grouped[:, :, part].reshape(slots.shape[0], col_count * chunk, B, B),
            "col",
            split_axis=1,
            concat_axis=0,
            tiled=True,
        )
        for part in range(CHUNKS)
    ]
    aux_local = chunk * CHUNKS
    pair_list = lax.dynamic_index_in_dim(block_pairs, row_index, 0, keepdims=False)
    selector = (pair_list[:, None] == jnp.arange(pair_total, dtype=jnp.int32)[None, :]).astype(
        jnp.bfloat16
    )
    full_mask = jnp.repeat(jnp.repeat(green_mask, B, axis=1), B, axis=2).astype(jnp.bfloat16)
    masked = greens * full_mask
    aux_total = dev_count * aux_local
    named_flag = (block_pairs >= 0).astype(jnp.int32)
    slot_index = jnp.arange(named_flag.shape[1], dtype=jnp.int32)
    not_later = (slot_index[None, :] <= slot_index[:, None]).astype(jnp.int32)
    position = jnp.sum(named_flag[:, None, :] * not_later[None, :, :], axis=2) - 1
    compact_hit = (position[:, None, :] == jnp.arange(NNZ, dtype=jnp.int32)[None, :, None]) & (
        named_flag[:, None, :] > 0
    )
    compact_sel = compact_hit.astype(jnp.int32)
    named_pairs = jnp.sum(compact_sel * block_pairs[:, None, :], axis=2)
    own_sel = lax.dynamic_index_in_dim(compact_sel, row_index, 0, keepdims=False).astype(
        jnp.bfloat16
    )
    block_span = B * B // dev_count
    expand = (
        named_pairs[:, :, None] == jnp.arange(pair_total, dtype=jnp.int32)[None, None, :]
    ).astype(jnp.bfloat16)
    image_parts, dense_parts = [], []
    for arrived in arrivals:
        x_compact = jnp.einsum(
            "js,sabc->ajbc", own_sel, arrived, preferred_element_type=jnp.float32
        ).astype(jnp.bfloat16)
        x_compact = x_compact.reshape(chunk, NNZ, dev_count, block_span)
        compact_rows = lax.all_to_all(
            x_compact, ("row", "col"), split_axis=2, concat_axis=0, tiled=True
        )
        pair_blocks = jnp.einsum(
            "kq,kabc->qabc", selector, arrived, preferred_element_type=jnp.float32
        ).astype(jnp.bfloat16)
        dense_x = pair_blocks.reshape(NBLK, NBLK, chunk, B, B).transpose(2, 0, 3, 1, 4)
        dense_x = dense_x.reshape(chunk, basis_count, basis_count)
        half_done = jnp.einsum(
            "ml,pmn->pln", masked[0], dense_x, preferred_element_type=jnp.float32
        ).astype(jnp.bfloat16)
        contracted = jnp.einsum(
            "pln,ns->pls", half_done, masked[1], preferred_element_type=jnp.float32
        ).astype(jnp.bfloat16)
        image_blocks = contracted.reshape(chunk, NBLK, B, NBLK, B).transpose(0, 1, 3, 2, 4)
        image_blocks = image_blocks.reshape(chunk, pair_total, dev_count, block_span)
        image_rows = lax.all_to_all(
            image_blocks, ("row", "col"), split_axis=2, concat_axis=0, tiled=True
        )
        compact_rows = compact_rows.reshape(row_count, col_count * chunk, NNZ, block_span)
        dense_rows = jnp.einsum(
            "rjk,rqjz->rqkz", expand, compact_rows, preferred_element_type=jnp.float32
        ).astype(jnp.bfloat16)
        image_rows = image_rows.reshape(dev_count, 1, chunk, pair_total * block_span)
        dense_rows = dense_rows.reshape(dev_count, 1, chunk, pair_total * block_span)
        image_parts.append(image_rows)
        dense_parts.append(dense_rows)
    image_rows = jnp.concatenate(image_parts, axis=1).reshape(aux_total, pair_total * block_span)
    dense_rows = jnp.concatenate(dense_parts, axis=1).reshape(aux_total, pair_total * block_span)
    chi_part = lax.dot_general(
        image_rows, dense_rows, (((1,), (1,)), ((), ())), preferred_element_type=jnp.float32
    )
    chi_parts = lax.all_to_all(
        chi_part.reshape(dev_count, aux_local, aux_total),
        ("row", "col"),
        split_axis=0,
        concat_axis=0,
        tiled=True,
    )
    chi_rows = jnp.sum(chi_parts, axis=0)
    column_mask = jnp.repeat(chi_mask[0], AB).astype(jnp.float32)
    return chi_rows * column_mask[None, :]


def solution(mesh):
    in_specs = (P("row", "col", None, None, None), P(), P(), P(), P("row", None))
    out_specs = P(("row", "col"), None)
    return jax.shard_map(
        on_device, mesh=mesh, in_specs=in_specs, out_specs=out_specs, check_vma=False
    )
```

```python
import jax
import jax.numpy as jnp
from jax import lax
from jax.sharding import PartitionSpec as P

B = 128
AB = 128
NBLK = 4
NNZ = 10
CHUNKS = 2


def on_device(x_slots, block_pairs, greens, green_mask, chi_mask):
    row_count = lax.axis_size("row")
    col_count = lax.axis_size("col")
    dev_count = row_count * col_count
    basis_count = NBLK * B
    pair_total = NBLK * NBLK
    row_index = lax.axis_index("row")
    slots = x_slots[0]
    chunk = slots.shape[1] // (col_count * CHUNKS)
    grouped = slots.reshape(slots.shape[0], col_count, CHUNKS, chunk, B, B)
    arrivals = [
        lax.all_to_all(
            grouped[:, :, part].reshape(slots.shape[0], col_count * chunk, B, B),
            "col",
            split_axis=1,
            concat_axis=0,
            tiled=True,
        )
        for part in range(CHUNKS)
    ]
    aux_local = chunk * CHUNKS
    pair_list = lax.dynamic_index_in_dim(block_pairs, row_index, 0, keepdims=False)
    selector = (pair_list[:, None] == jnp.arange(pair_total, dtype=jnp.int32)[None, :]).astype(
        jnp.bfloat16
    )
    full_mask = jnp.repeat(jnp.repeat(green_mask, B, axis=1), B, axis=2).astype(jnp.bfloat16)
    masked = greens * full_mask
    aux_total = dev_count * aux_local
    named_flag = (block_pairs >= 0).astype(jnp.int32)
    slot_index = jnp.arange(named_flag.shape[1], dtype=jnp.int32)
    not_later = (slot_index[None, :] <= slot_index[:, None]).astype(jnp.int32)
    position = jnp.sum(named_flag[:, None, :] * not_later[None, :, :], axis=2) - 1
    compact_hit = (position[:, None, :] == jnp.arange(NNZ, dtype=jnp.int32)[None, :, None]) & (
        named_flag[:, None, :] > 0
    )
    compact_sel = compact_hit.astype(jnp.int32)
    named_pairs = jnp.sum(compact_sel * block_pairs[:, None, :], axis=2)
    own_sel = lax.dynamic_index_in_dim(compact_sel, row_index, 0, keepdims=False).astype(
        jnp.bfloat16
    )
    block_span = B * B // dev_count
    expand = (
        named_pairs[:, :, None] == jnp.arange(pair_total, dtype=jnp.int32)[None, None, :]
    ).astype(jnp.bfloat16)
    image_parts, dense_parts = [], []
    for arrived in arrivals:
        x_compact = jnp.einsum(
            "js,sabc->ajbc", own_sel, arrived, preferred_element_type=jnp.float32
        ).astype(jnp.bfloat16)
        x_compact = x_compact.reshape(chunk, NNZ, dev_count, block_span)
        compact_rows = lax.all_to_all(
            x_compact, ("row", "col"), split_axis=2, concat_axis=0, tiled=True
        )
        pair_blocks = jnp.einsum(
            "kq,kabc->qabc", selector, arrived, preferred_element_type=jnp.float32
        ).astype(jnp.bfloat16)
        dense_x = pair_blocks.reshape(NBLK, NBLK, chunk, B, B).transpose(2, 0, 3, 1, 4)
        dense_x = dense_x.reshape(chunk, basis_count, basis_count)
        half_done = jnp.einsum(
            "ml,pmn->pln", masked[0], dense_x, preferred_element_type=jnp.float32
        ).astype(jnp.bfloat16)
        contracted = jnp.einsum(
            "pln,ns->pls", half_done, masked[1], preferred_element_type=jnp.float32
        ).astype(jnp.bfloat16)
        image_blocks = contracted.reshape(chunk, NBLK, B, NBLK, B).transpose(0, 1, 3, 2, 4)
        image_blocks = image_blocks.reshape(chunk, pair_total, dev_count, block_span)
        image_rows = lax.all_to_all(
            image_blocks, ("row", "col"), split_axis=2, concat_axis=0, tiled=True
        )
        compact_rows = compact_rows.reshape(row_count, col_count * chunk, NNZ, block_span)
        dense_rows = jnp.einsum(
            "rjk,rqjz->rqkz", expand, compact_rows, preferred_element_type=jnp.float32
        ).astype(jnp.bfloat16)
        image_rows = image_rows.reshape(dev_count, 1, chunk, pair_total * block_span)
        dense_rows = dense_rows.reshape(dev_count, 1, chunk, pair_total * block_span)
        image_parts.append(image_rows)
        dense_parts.append(dense_rows)
    dense_rows = jnp.concatenate(dense_parts, axis=1).reshape(aux_total, pair_total * block_span)
    chi_sums = []
    for image_rows in image_parts:
        chi_part = lax.dot_general(
            image_rows.reshape(dev_count * chunk, pair_total * block_span),
            dense_rows,
            (((1,), (1,)), ((), ())),
            preferred_element_type=jnp.float32,
        )
        chi_parts = lax.all_to_all(
            chi_part.reshape(dev_count, chunk, aux_total),
            ("row", "col"),
            split_axis=0,
            concat_axis=0,
            tiled=True,
        )
        chi_sums.append(jnp.sum(chi_parts, axis=0))
    chi_rows = jnp.concatenate(chi_sums, axis=0)
    column_mask = jnp.repeat(chi_mask[0], AB).astype(jnp.float32)
    return chi_rows * column_mask[None, :]


def solution(mesh):
    in_specs = (P("row", "col", None, None, None), P(), P(), P(), P("row", None))
    out_specs = P(("row", "col"), None)
    return jax.shard_map(
        on_device, mesh=mesh, in_specs=in_specs, out_specs=out_specs, check_vma=False
    )
```

```python
import jax
import jax.numpy as jnp
from jax import lax
from jax.sharding import PartitionSpec as P

B = 128
AB = 128
NBLK = 4
NNZ = 10
CHUNKS = 2


def on_device(x_slots, block_pairs, greens, green_mask, chi_mask):
    row_count = lax.axis_size("row")
    col_count = lax.axis_size("col")
    dev_count = row_count * col_count
    basis_count = NBLK * B
    pair_total = NBLK * NBLK
    row_index = lax.axis_index("row")
    slots = x_slots[0]
    chunk = slots.shape[1] // (col_count * CHUNKS)
    group = col_count * chunk
    arrivals = [
        lax.all_to_all(
            slots[:, part * group : (part + 1) * group],
            "col",
            split_axis=1,
            concat_axis=0,
            tiled=True,
        )
        for part in range(CHUNKS)
    ]
    aux_local = chunk * CHUNKS
    pair_list = lax.dynamic_index_in_dim(block_pairs, row_index, 0, keepdims=False)
    selector = (pair_list[:, None] == jnp.arange(pair_total, dtype=jnp.int32)[None, :]).astype(
        jnp.bfloat16
    )
    full_mask = jnp.repeat(jnp.repeat(green_mask, B, axis=1), B, axis=2).astype(jnp.bfloat16)
    masked = greens * full_mask
    aux_total = dev_count * aux_local
    named_flag = (block_pairs >= 0).astype(jnp.int32)
    slot_index = jnp.arange(named_flag.shape[1], dtype=jnp.int32)
    not_later = (slot_index[None, :] <= slot_index[:, None]).astype(jnp.int32)
    position = jnp.sum(named_flag[:, None, :] * not_later[None, :, :], axis=2) - 1
    compact_hit = (position[:, None, :] == jnp.arange(NNZ, dtype=jnp.int32)[None, :, None]) & (
        named_flag[:, None, :] > 0
    )
    compact_sel = compact_hit.astype(jnp.int32)
    named_pairs = jnp.sum(compact_sel * block_pairs[:, None, :], axis=2)
    own_sel = lax.dynamic_index_in_dim(compact_sel, row_index, 0, keepdims=False).astype(
        jnp.bfloat16
    )
    block_span = B * B // dev_count
    expand = (
        named_pairs[:, :, None] == jnp.arange(pair_total, dtype=jnp.int32)[None, None, :]
    ).astype(jnp.bfloat16)
    image_parts, dense_parts = [], []
    for arrived in arrivals:
        x_compact = jnp.einsum(
            "js,sabc->ajbc", own_sel, arrived, preferred_element_type=jnp.float32
        ).astype(jnp.bfloat16)
        x_compact = x_compact.reshape(chunk, NNZ, dev_count, block_span)
        compact_rows = lax.all_to_all(
            x_compact, ("row", "col"), split_axis=2, concat_axis=0, tiled=True
        )
        pair_blocks = jnp.einsum(
            "kq,kabc->qabc", selector, arrived, preferred_element_type=jnp.float32
        ).astype(jnp.bfloat16)
        dense_x = pair_blocks.reshape(NBLK, NBLK, chunk, B, B).transpose(2, 0, 3, 1, 4)
        dense_x = dense_x.reshape(chunk, basis_count, basis_count)
        half_done = jnp.einsum(
            "ml,pmn->pln", masked[0], dense_x, preferred_element_type=jnp.float32
        ).astype(jnp.bfloat16)
        contracted = jnp.einsum(
            "pln,ns->pls", half_done, masked[1], preferred_element_type=jnp.float32
        ).astype(jnp.bfloat16)
        image_blocks = contracted.reshape(chunk, NBLK, B, NBLK, B).transpose(0, 1, 3, 2, 4)
        image_blocks = image_blocks.reshape(chunk, pair_total, dev_count, block_span)
        image_rows = lax.all_to_all(
            image_blocks, ("row", "col"), split_axis=2, concat_axis=0, tiled=True
        )
        compact_rows = compact_rows.reshape(row_count, group, NNZ, block_span)
        dense_rows = jnp.einsum(
            "rjk,rqjz->rqkz", expand, compact_rows, preferred_element_type=jnp.float32
        ).astype(jnp.bfloat16)
        image_rows = image_rows.reshape(row_count, 1, group, pair_total * block_span)
        dense_rows = dense_rows.reshape(row_count, 1, group, pair_total * block_span)
        image_parts.append(image_rows)
        dense_parts.append(dense_rows)
    dense_rows = jnp.concatenate(dense_parts, axis=1).reshape(aux_total, pair_total * block_span)
    chi_sums = []
    for image_rows in image_parts:
        chi_part = lax.dot_general(
            image_rows.reshape(row_count * group, pair_total * block_span),
            dense_rows,
            (((1,), (1,)), ((), ())),
            preferred_element_type=jnp.float32,
        )
        row_parts = lax.all_to_all(
            chi_part.reshape(row_count, group, aux_total),
            "row",
            split_axis=0,
            concat_axis=0,
            tiled=True,
        )
        chi_sums.append(jnp.sum(row_parts, axis=0))
    chi_parts = lax.all_to_all(
        jnp.concatenate(chi_sums, axis=0).reshape(col_count, aux_local, aux_total),
        "col",
        split_axis=0,
        concat_axis=0,
        tiled=True,
    )
    chi_rows = jnp.sum(chi_parts, axis=0)
    column_mask = jnp.repeat(chi_mask[0], AB).astype(jnp.float32)
    return chi_rows * column_mask[None, :]


def solution(mesh):
    in_specs = (P("row", "col", None, None, None), P(), P(), P(), P("row", None))
    out_specs = P(("row", "col"), None)
    return jax.shard_map(
        on_device, mesh=mesh, in_specs=in_specs, out_specs=out_specs, check_vma=False
    )
```

```python
import jax
import jax.numpy as jnp
from jax import lax
from jax.sharding import PartitionSpec as P

B = 128
AB = 128
NBLK = 4
NNZ = 10
CHUNKS = 2


def on_device(x_slots, block_pairs, greens, green_mask, chi_mask):
    row_count = lax.axis_size("row")
    col_count = lax.axis_size("col")
    dev_count = row_count * col_count
    basis_count = NBLK * B
    pair_total = NBLK * NBLK
    row_index = lax.axis_index("row")
    slots = x_slots[0]
    chunk = slots.shape[1] // (col_count * CHUNKS)
    grouped = slots.reshape(slots.shape[0], col_count, CHUNKS, chunk, B, B)
    arrivals = [
        lax.all_to_all(
            grouped[:, :, part].reshape(slots.shape[0], col_count * chunk, B, B),
            "col",
            split_axis=1,
            concat_axis=0,
            tiled=True,
        )
        for part in range(CHUNKS)
    ]
    aux_local = chunk * CHUNKS
    pair_list = lax.dynamic_index_in_dim(block_pairs, row_index, 0, keepdims=False)
    selector = (pair_list[:, None] == jnp.arange(pair_total, dtype=jnp.int32)[None, :]).astype(
        jnp.bfloat16
    )
    full_mask = jnp.repeat(jnp.repeat(green_mask, B, axis=1), B, axis=2).astype(jnp.bfloat16)
    masked = greens * full_mask
    aux_total = dev_count * aux_local
    named_flag = (block_pairs >= 0).astype(jnp.int32)
    slot_index = jnp.arange(named_flag.shape[1], dtype=jnp.int32)
    not_later = (slot_index[None, :] <= slot_index[:, None]).astype(jnp.int32)
    position = jnp.sum(named_flag[:, None, :] * not_later[None, :, :], axis=2) - 1
    compact_hit = (position[:, None, :] == jnp.arange(NNZ, dtype=jnp.int32)[None, :, None]) & (
        named_flag[:, None, :] > 0
    )
    compact_sel = compact_hit.astype(jnp.int32)
    named_pairs = jnp.sum(compact_sel * block_pairs[:, None, :], axis=2)
    own_sel = lax.dynamic_index_in_dim(compact_sel, row_index, 0, keepdims=False).astype(
        jnp.bfloat16
    )
    block_span = B * B // dev_count
    expand = (
        named_pairs[:, :, None] == jnp.arange(pair_total, dtype=jnp.int32)[None, None, :]
    ).astype(jnp.bfloat16)
    image_parts, dense_parts = [], []
    for arrived in arrivals:
        x_compact = jnp.einsum(
            "js,sabc->ajbc", own_sel, arrived, preferred_element_type=jnp.float32
        ).astype(jnp.bfloat16)
        x_compact = x_compact.reshape(chunk, NNZ, dev_count, block_span)
        compact_rows = lax.all_to_all(
            x_compact, ("row", "col"), split_axis=2, concat_axis=0, tiled=True
        )
        pair_blocks = jnp.einsum(
            "kq,kabc->qabc", selector, arrived, preferred_element_type=jnp.float32
        ).astype(jnp.bfloat16)
        dense_x = pair_blocks.reshape(NBLK, NBLK, chunk, B, B).transpose(2, 0, 3, 1, 4)
        dense_x = dense_x.reshape(chunk, basis_count, basis_count)
        half_done = jnp.einsum(
            "ml,pmn->pln", masked[0], dense_x, preferred_element_type=jnp.float32
        ).astype(jnp.bfloat16)
        contracted = jnp.einsum(
            "pln,ns->pls", half_done, masked[1], preferred_element_type=jnp.float32
        ).astype(jnp.bfloat16)
        image_blocks = contracted.reshape(chunk, NBLK, B, NBLK, B).transpose(0, 1, 3, 2, 4)
        image_blocks = image_blocks.reshape(chunk, pair_total, dev_count, block_span)
        image_blocks = image_blocks.transpose(2, 1, 0, 3)
        image_rows = lax.all_to_all(
            image_blocks, ("row", "col"), split_axis=0, concat_axis=0, tiled=True
        )
        compact_rows = compact_rows.reshape(row_count, col_count * chunk, NNZ, block_span)
        dense_rows = jnp.einsum(
            "rjk,rqjz->rqkz", expand, compact_rows, preferred_element_type=jnp.float32
        ).astype(jnp.bfloat16)
        dense_rows = dense_rows.reshape(dev_count, 1, chunk, pair_total * block_span)
        image_parts.append(image_rows)
        dense_parts.append(dense_rows)
    dense_rows = jnp.concatenate(dense_parts, axis=1).reshape(aux_total, pair_total * block_span)
    chi_sums = []
    for image_rows in image_parts:
        chi_part = sum(
            jnp.einsum(
                "diz,qz->diq",
                image_rows[:, pair],
                dense_rows[:, pair * block_span : (pair + 1) * block_span],
                preferred_element_type=jnp.float32,
            )
            for pair in range(pair_total)
        )
        chi_parts = lax.all_to_all(
            chi_part.reshape(dev_count, chunk, aux_total),
            ("row", "col"),
            split_axis=0,
            concat_axis=0,
            tiled=True,
        )
        chi_sums.append(jnp.sum(chi_parts, axis=0))
    chi_rows = jnp.concatenate(chi_sums, axis=0)
    column_mask = jnp.repeat(chi_mask[0], AB).astype(jnp.float32)
    return chi_rows * column_mask[None, :]


def solution(mesh):
    in_specs = (P("row", "col", None, None, None), P(), P(), P(), P("row", None))
    out_specs = P(("row", "col"), None)
    return jax.shard_map(
        on_device, mesh=mesh, in_specs=in_specs, out_specs=out_specs, check_vma=False
    )
```
